32 devices in a mesh: groups: 2 (over y), tm: 4 (over z), space: 4 (over x, core).
Axes of the slice: x: 2, y: 2, z: 4, core: 2. Of those that a mesh axis runs over, the one named last changes fastest.
Arguments:
- solution: float32 [8, 16, 128, 128], P(('groups', 'tm'), 'space'), parts along dimension 0, may hold values from -6 to 6
- residual: float32 [8, 16, 128, 128], P(('groups', 'tm'), 'space'), parts along dimension 0, may hold values from -6 to 6
- direction: float32 [8, 16, 128, 128], P(('groups', 'tm'), 'space'), parts along dimension 0, may hold values from -6 to 6
- capacity: float32 [32, 128, 128], P(('groups', 'space')), parts along dimension 0, may hold values from 0.5 to 8
Outputs:
- new_solution: float32 [8, 16, 128, 128], P(('groups', 'tm'), 'space'), parts along dimension 0
- new_residual: float32 [8, 16, 128, 128], P(('groups', 'tm'), 'space'), parts along dimension 0
- new_direction: float32 [8, 16, 128, 128], P(('groups', 'tm'), 'space'), parts along dimension 0
The draws below stay inside these ranges and needn't reach their ends.
There are 2 independent parts, one for each index of `groups`. The reference program is written for one: setup_inputs(seed, part) draws one part's arguments, and reference() takes and returns one part's arrays. A program takes and returns all parts, laid end to end along the dimension named above; each array names one. Nothing has to cross between parts.
All inputs are finite; a program needn't handle non-finite values.
Results may differ from the reference program's by a relative error of at most 0.000038.
Values sent between devices are 32-bit elements; how exact they have to be, the bound alone decides.
A program may use at most 64 MiB of HBM per device.

```python
import math
import jax
import jax.numpy as jnp

NX = 128
NY = 128
STEPS = 4
NZ = 16


def block_scale(stream_key, extent, split, smallest, high):
    def one(position, blocks):
        draws = jax.random.uniform(jax.random.fold_in(jax.random.fold_in(stream_key, 6), position), (blocks,), jnp.float32, smallest / len(split), high / len(split))
        return jnp.repeat(jnp.exp(draws), extent[position] // blocks).reshape((-1,) + (1,) * (len(extent) - position - 1))

    factor_of = one(*split[0])
    for cut in split[1:]:
        factor_of = factor_of * one(*cut)
    return factor_of


def gaussian(stream_key, extent, scale, reach, cuts=(), dtype=jnp.bfloat16):
    entries = jax.random.normal(stream_key, extent, jnp.float32) * scale
    if len(cuts) > 0:
        entries = block_scale(stream_key, extent, cuts, -0.22, 0.18) * entries
    return jnp.clip(entries, min=-reach, max=reach).astype(dtype)


def setup_inputs(seed: int = 0, part: int = 0) -> dict:
    key_list = jax.random.split(jax.random.key(seed), 5)
    part_splits = jax.random.split(jax.random.fold_in(key_list[4], part), 5)
    solution = gaussian(part_splits[0], (STEPS, NZ, NX, NY), 1.0, 6.0, ((0, 4), (1, 4)), jnp.float32)
    residual = gaussian(part_splits[1], (STEPS, NZ, NX, NY), 1.0, 6.0, ((0, 4), (1, 4)), jnp.float32)
    direction = gaussian(part_splits[2], (STEPS, NZ, NX, NY), 1.0, 6.0, ((0, 4), (1, 4)), jnp.float32)
    capacity = jnp.clip(jnp.exp(math.log(8.0) - 2.7725887 * jax.random.uniform(part_splits[3], (NZ, NX, NY), jnp.float32) ** block_scale(part_splits[3], (NZ, NX, NY), ((0, 4),), -0.2, 0.2)), 0.5, 8.0)
    return dict(solution=solution, residual=residual, direction=direction, capacity=capacity)


def spatial(values, capacity):
    padded = jnp.pad(values, ((0, 0), (1, 1), (1, 1), (1, 1)))
    beside = padded[:, 2:, 1:-1, 1:-1] + padded[:, :-2, 1:-1, 1:-1]
    beside = beside + padded[:, 1:-1, 2:, 1:-1] + padded[:, 1:-1, :-2, 1:-1]
    beside = beside + padded[:, 1:-1, 1:-1, 2:] + padded[:, 1:-1, 1:-1, :-2]
    return (6.0 + capacity) * values - beside


def forward_op(values, capacity):
    previous = jnp.concatenate([jnp.zeros_like(values[:1]), values[:-1]], axis=0)
    return spatial(values, capacity) - capacity * previous


def backward_op(values, capacity):
    following = jnp.concatenate([values[1:], jnp.zeros_like(values[:1])], axis=0)
    return spatial(values, capacity) - capacity * following


def reference(solution, residual, direction, capacity):
    gradient = backward_op(residual, capacity)
    grad_norm = jnp.sum(gradient * gradient)
    image_field = forward_op(direction, capacity)
    image_norm = jnp.sum(image_field * image_field)
    step_size = grad_norm / image_norm
    new_solution = solution + step_size * direction
    new_residual = residual - step_size * image_field
    new_gradient = backward_op(new_residual, capacity)
    new_norm = jnp.sum(new_gradient * new_gradient)
    new_direction = new_gradient + (new_norm / grad_norm) * direction
    return new_solution, new_residual, new_direction
```

```python
import functools

import jax
import jax.numpy as jnp
from jax import lax
from jax.experimental import pallas as pl
from jax.experimental.pallas import tpu as pltpu
from jax.sharding import PartitionSpec as P

MESH = pl.DeviceIdType.MESH


def beside(v, up, down):
    nx, ny = v.shape
    row = lax.broadcasted_iota(jnp.int32, v.shape, 0)
    col = lax.broadcasted_iota(jnp.int32, v.shape, 1)
    total = up + down
    total = total + jnp.where(row == 0, 0.0, pltpu.roll(v, 1, 0))
    total = total + jnp.where(row == nx - 1, 0.0, pltpu.roll(v, nx - 1, 0))
    total = total + jnp.where(col == 0, 0.0, pltpu.roll(v, 1, 1))
    return total + jnp.where(col == ny - 1, 0.0, pltpu.roll(v, ny - 1, 1))


def spatial(ref, halo, capacity, k):
    last = ref.shape[0] - 1
    v = ref[k]
    up = ref[k - 1] if k > 0 else halo[0]
    down = ref[k + 1] if k < last else halo[1]
    return (6.0 + capacity) * v - beside(v, up, down)


def folded(x):
    return jnp.sum(x, axis=0, keepdims=True)


def exchange(
    T, S, r_in, d_in, c_in, a_out, g_out, w_out, coef,
    rv, dv, cv, rn, dp, an, zr, zd, za, av, gv, wv, stats,
    in_sem, out_sem, t_send, t_recv, z_send, z_recv, s_send, s_recv,
):
    L = rv.shape[0]
    N = T * S
    t, s = lax.axis_index("tm"), lax.axis_index("space")
    me = t * S + s
    earlier, later = t > 0, t < T - 1
    lower, upper = s > 0, s < S - 1

    loads = [
        pltpu.make_async_copy(src, dst, in_sem.at[i])
        for i, (src, dst) in enumerate(((d_in, dv), (r_in, rv), (c_in, cv)))
    ]
    for load in loads:
        load.start()

    def peer(o):
        other = lax.rem(me + o, N)
        return {"tm": lax.div(other, S), "space": lax.rem(other, S)}

    def each_peer(do):
        if N <= 16:
            for o in range(1, N):
                do(o)
        else:
            def body(o, carry):
                do(o)
                return carry
            lax.fori_loop(1, N, body, 0)

    barrier = pltpu.get_barrier_semaphore()
    each_peer(lambda o: pl.semaphore_signal(barrier, inc=1, device_id=peer(o), device_id_type=MESH))

    @pl.when(jnp.logical_not(earlier))
    def _():
        dp[...] = jnp.zeros_like(dp)

    @pl.when(jnp.logical_not(later))
    def _():
        rn[...] = jnp.zeros_like(rn)
        an[...] = jnp.zeros_like(an)

    @pl.when(jnp.logical_not(lower))
    def _():
        for z in (zr, zd, za):
            z[0] = jnp.zeros(z.shape[1:], z.dtype)

    @pl.when(jnp.logical_not(upper))
    def _():
        for z in (zr, zd, za):
            z[1] = jnp.zeros(z.shape[1:], z.dtype)

    pl.semaphore_wait(barrier, N - 1)

    def step_copy(i, src, dst, k, to):
        return pltpu.make_async_remote_copy(
            src_ref=src.at[k], dst_ref=dst.at[k], send_sem=t_send.at[i, k], recv_sem=t_recv.at[i, k],
            device_id={"tm": to}, device_id_type=MESH)

    def layer_copy(i, src, dst, up):
        return pltpu.make_async_remote_copy(
            src_ref=src.at[L - 1 if up else 0], dst_ref=dst.at[0 if up else 1],
            send_sem=z_send.at[i, 0 if up else 1], recv_sem=z_recv.at[i, 0 if up else 1],
            device_id={"space": s + 1 if up else s - 1}, device_id_type=MESH)

    d_step = [step_copy(0, d_in, dp, k, t + 1) for k in range(L)]
    r_step = [step_copy(1, r_in, rn, k, t - 1) for k in range(L)]
    a_step = [step_copy(2, av, an, k, t - 1) for k in range(L)]
    d_up, d_down = layer_copy(0, d_in, zd, True), layer_copy(0, d_in, zd, False)
    r_up, r_down = layer_copy(1, r_in, zr, True), layer_copy(1, r_in, zr, False)
    a_up, a_down = layer_copy(2, av, za, True), layer_copy(2, av, za, False)

    @pl.when(upper)
    def _():
        d_up.start()

    @pl.when(lower)
    def _():
        d_down.start()

    @pl.when(later)
    def _():
        for copy in d_step:
            copy.start()

    @pl.when(earlier)
    def _():
        for copy in r_step:
            copy.start()

    @pl.when(upper)
    def _():
        r_up.start()

    @pl.when(lower)
    def _():
        r_down.start()

    def arrive(when, copy):
        @pl.when(when)
        def _():
            copy.wait_recv()

    for load in loads:
        load.wait()
    arrive(lower, d_up)
    arrive(upper, d_down)
    aa = jnp.zeros((1, cv.shape[2]), jnp.float32)
    for k in range(L):
        part = spatial(dv, zd, cv[k], k)
        arrive(earlier, d_step[k])
        image = part - cv[k] * dp[k]
        av[k] = image
        aa = aa + folded(image * image)

        @pl.when(earlier)
        def _():
            a_step[k].start()

        if k == 0:
            @pl.when(lower)
            def _():
                a_down.start()
        if k == L - 1:
            @pl.when(upper)
            def _():
                a_up.start()
    write_a = pltpu.make_async_copy(av, a_out, out_sem.at[0])
    write_a.start()

    arrive(lower, r_up)
    arrive(upper, r_down)
    gg = jnp.zeros((1, cv.shape[2]), jnp.float32)
    for k in range(L):
        part = spatial(rv, zr, cv[k], k)
        arrive(later, r_step[k])
        gradient = part - cv[k] * rn[k]
        gv[k] = gradient
        gg = gg + folded(gradient * gradient)
    write_g = pltpu.make_async_copy(gv, g_out, out_sem.at[1])
    write_g.start()

    arrive(lower, a_up)
    arrive(upper, a_down)
    gw = jnp.zeros((1, cv.shape[2]), jnp.float32)
    ww = jnp.zeros((1, cv.shape[2]), jnp.float32)
    for k in range(L):
        wv[k] = spatial(av, za, cv[k], k)
    for k in range(L):
        arrive(later, a_step[k])
        change = wv[k] - cv[k] * an[k]
        wv[k] = change
        gw = gw + folded(gv[k] * change)
        ww = ww + folded(change * change)

    stats[me] = jnp.concatenate([gg, aa, gw, ww, gg, aa, gw, ww], axis=0)

    def stat_copy(o):
        return pltpu.make_async_remote_copy(
            src_ref=stats.at[me], dst_ref=stats.at[me], send_sem=s_send.at[o], recv_sem=s_recv.at[me],
            device_id=peer(o), device_id_type=MESH)

    def stat_wait(o):
        other = lax.rem(me + o, N)
        pltpu.make_async_remote_copy(
            src_ref=stats.at[other], dst_ref=stats.at[other], send_sem=s_send.at[o], recv_sem=s_recv.at[other],
            device_id=peer(o), device_id_type=MESH).wait_recv()

    each_peer(lambda o: stat_copy(o).start())
    write_w = pltpu.make_async_copy(wv, w_out, out_sem.at[2])
    write_w.start()
    each_peer(stat_wait)

    whole = jnp.sum(jnp.sum(stats[...], axis=0), axis=1, keepdims=True)
    whole = jnp.broadcast_to(whole, (8, coef.shape[1]))
    grad_norm, image_norm, cross, change_norm = (whole[i:i + 1] for i in range(4))
    step_size = grad_norm / image_norm
    new_norm = grad_norm + step_size * (step_size * change_norm - 2.0 * cross)
    ratio = new_norm / grad_norm
    coef[...] = jnp.concatenate([step_size, ratio] * 4, axis=0)

    def sent(when, *copies):
        @pl.when(when)
        def _():
            for copy in copies:
                copy.wait_send()

    sent(later, *d_step)
    sent(earlier, *r_step, *a_step)
    sent(upper, d_up, r_up, a_up)
    sent(lower, d_down, r_down, a_down)
    each_peer(lambda o: stat_copy(o).wait_send())
    for write in (write_a, write_g, write_w):
        write.wait()


def local(T, S, solution, residual, direction, capacity):
    L, X, Y = capacity.shape
    field = jax.ShapeDtypeStruct((L, X, Y), jnp.float32)
    whole = pltpu.VMEM((L, X, Y), jnp.float32)
    halo = pltpu.VMEM((2, X, Y), jnp.float32)
    image, gradient, change, coef = pl.pallas_call(
        functools.partial(exchange, T, S),
        out_shape=(field, field, field, jax.ShapeDtypeStruct((8, Y), jnp.float32)),
        in_specs=[pl.BlockSpec(memory_space=pl.ANY)] * 3,
        out_specs=(pl.BlockSpec(memory_space=pl.ANY),) * 3 + (pl.BlockSpec(memory_space=pltpu.VMEM),),
        scratch_shapes=[whole] * 6 + [halo] * 3 + [whole] * 3 + [
            pltpu.VMEM((T * S, 8, Y), jnp.float32),
            pltpu.SemaphoreType.DMA((3,)),
            pltpu.SemaphoreType.DMA((3,)),
            pltpu.SemaphoreType.DMA((3, L)),
            pltpu.SemaphoreType.DMA((3, L)),
            pltpu.SemaphoreType.DMA((3, 2)),
            pltpu.SemaphoreType.DMA((3, 2)),
            pltpu.SemaphoreType.DMA((T * S,)),
            pltpu.SemaphoreType.DMA((T * S,)),
        ],
        compiler_params=pltpu.CompilerParams(
            collective_id=0, has_side_effects=True, vmem_limit_bytes=16 * 1024 * 1024),
    )(residual[0], direction[0], capacity)
    step_size, ratio = coef[0, 0], coef[1, 0]
    new_solution = solution + step_size * direction
    new_residual = residual - step_size * image[None]
    new_direction = gradient[None] - step_size * change[None] + ratio * direction
    return new_solution, new_residual, new_direction


def solution(mesh):
    field = P(("groups", "tm"), "space", None, None)
    return jax.shard_map(
        functools.partial(local, mesh.shape["tm"], mesh.shape["space"]),
        mesh=mesh,
        in_specs=(field, field, field, P(("groups", "space"), None, None)),
        out_specs=(field, field, field),
        check_vma=False,
    )
```

```python
import functools

import jax
import jax.numpy as jnp
from jax import lax
from jax.experimental import pallas as pl
from jax.experimental.pallas import tpu as pltpu
from jax.sharding import PartitionSpec as P

MESH = pl.DeviceIdType.MESH


def beside(v, up, down):
    nx, ny = v.shape
    row = lax.broadcasted_iota(jnp.int32, v.shape, 0)
    col = lax.broadcasted_iota(jnp.int32, v.shape, 1)
    total = up + down
    total = total + jnp.where(row == 0, 0.0, pltpu.roll(v, 1, 0))
    total = total + jnp.where(row == nx - 1, 0.0, pltpu.roll(v, nx - 1, 0))
    total = total + jnp.where(col == 0, 0.0, pltpu.roll(v, 1, 1))
    return total + jnp.where(col == ny - 1, 0.0, pltpu.roll(v, ny - 1, 1))


def spatial(ref, halo, capacity, k):
    last = ref.shape[0] - 1
    v = ref[k]
    up = ref[k - 1] if k > 0 else halo[0]
    down = ref[k + 1] if k < last else halo[1]
    return (6.0 + capacity) * v - beside(v, up, down)


def folded(x):
    return jnp.sum(x, axis=0, keepdims=True)


def exchange(
    T, S, x_in, r_in, d_in, c_in, xv, rv, dv, av, gv, wv, coef,
    cv, rn, dp, an, zr, zd, za, stats,
    in_sem, t_send, t_recv, z_send, z_recv, s_send, s_recv,
):
    L = rv.shape[0]
    N = T * S
    t, s = lax.axis_index("tm"), lax.axis_index("space")
    me = t * S + s
    earlier, later = t > 0, t < T - 1
    lower, upper = s > 0, s < S - 1

    loads = [
        pltpu.make_async_copy(src, dst, in_sem.at[i])
        for i, (src, dst) in enumerate(((d_in, dv), (c_in, cv), (r_in, rv), (x_in, xv)))
    ]
    for load in loads:
        load.start()

    def peer(o):
        other = lax.rem(me + o, N)
        return {"tm": lax.div(other, S), "space": lax.rem(other, S)}

    def each_peer(do):
        if N <= 16:
            for o in range(1, N):
                do(o)
        else:
            def body(o, carry):
                do(o)
                return carry
            lax.fori_loop(1, N, body, 0)

    barrier = pltpu.get_barrier_semaphore()
    each_peer(lambda o: pl.semaphore_signal(barrier, inc=1, device_id=peer(o), device_id_type=MESH))

    @pl.when(jnp.logical_not(earlier))
    def _():
        dp[...] = jnp.zeros_like(dp)

    @pl.when(jnp.logical_not(later))
    def _():
        rn[...] = jnp.zeros_like(rn)
        an[...] = jnp.zeros_like(an)

    @pl.when(jnp.logical_not(lower))
    def _():
        for z in (zr, zd, za):
            z[0] = jnp.zeros(z.shape[1:], z.dtype)

    @pl.when(jnp.logical_not(upper))
    def _():
        for z in (zr, zd, za):
            z[1] = jnp.zeros(z.shape[1:], z.dtype)

    pl.semaphore_wait(barrier, N - 1)

    def step_copy(i, src, dst, k, to):
        return pltpu.make_async_remote_copy(
            src_ref=src.at[k], dst_ref=dst.at[k], send_sem=t_send.at[i, k], recv_sem=t_recv.at[i, k],
            device_id={"tm": to}, device_id_type=MESH)

    def layer_copy(i, src, dst, up):
        return pltpu.make_async_remote_copy(
            src_ref=src.at[L - 1 if up else 0], dst_ref=dst.at[0 if up else 1],
            send_sem=z_send.at[i, 0 if up else 1], recv_sem=z_recv.at[i, 0 if up else 1],
            device_id={"space": s + 1 if up else s - 1}, device_id_type=MESH)

    d_step = [step_copy(0, d_in, dp, k, t + 1) for k in range(L)]
    r_step = [step_copy(1, r_in, rn, k, t - 1) for k in range(L)]
    a_step = [step_copy(2, av, an, k, t - 1) for k in range(L)]
    d_up, d_down = layer_copy(0, d_in, zd, True), layer_copy(0, d_in, zd, False)
    r_up, r_down = layer_copy(1, r_in, zr, True), layer_copy(1, r_in, zr, False)
    a_up, a_down = layer_copy(2, av, za, True), layer_copy(2, av, za, False)

    @pl.when(upper)
    def _():
        d_up.start()

    @pl.when(lower)
    def _():
        d_down.start()

    @pl.when(later)
    def _():
        for copy in d_step:
            copy.start()

    @pl.when(earlier)
    def _():
        for copy in r_step:
            copy.start()

    @pl.when(upper)
    def _():
        r_up.start()

    @pl.when(lower)
    def _():
        r_down.start()

    def arrive(when, copy):
        @pl.when(when)
        def _():
            copy.wait_recv()

    for load in loads:
        load.wait()
    arrive(lower, d_up)
    arrive(upper, d_down)
    aa = jnp.zeros((1, cv.shape[2]), jnp.float32)
    for k in range(L):
        part = spatial(dv, zd, cv[k], k)
        arrive(earlier, d_step[k])
        image = part - cv[k] * dp[k]
        av[k] = image
        aa = aa + folded(image * image)

        @pl.when(earlier)
        def _():
            a_step[k].start()

        if k == 0:
            @pl.when(lower)
            def _():
                a_down.start()
        if k == L - 1:
            @pl.when(upper)
            def _():
                a_up.start()

    arrive(lower, r_up)
    arrive(upper, r_down)
    gg = jnp.zeros((1, cv.shape[2]), jnp.float32)
    for k in range(L):
        part = spatial(rv, zr, cv[k], k)
        arrive(later, r_step[k])
        gradient = part - cv[k] * rn[k]
        gv[k] = gradient
        gg = gg + folded(gradient * gradient)

    arrive(lower, a_up)
    arrive(upper, a_down)
    gw = jnp.zeros((1, cv.shape[2]), jnp.float32)
    ww = jnp.zeros((1, cv.shape[2]), jnp.float32)
    for k in range(L):
        wv[k] = spatial(av, za, cv[k], k)
    for k in range(L):
        arrive(later, a_step[k])
        change = wv[k] - cv[k] * an[k]
        wv[k] = change
        gw = gw + folded(gv[k] * change)
        ww = ww + folded(change * change)

    stats[me] = jnp.concatenate([gg, aa, gw, ww, gg, aa, gw, ww], axis=0)

    def stat_copy(o):
        return pltpu.make_async_remote_copy(
            src_ref=stats.at[me], dst_ref=stats.at[me], send_sem=s_send.at[o], recv_sem=s_recv.at[me],
            device_id=peer(o), device_id_type=MESH)

    def stat_wait(o):
        other = lax.rem(me + o, N)
        pltpu.make_async_remote_copy(
            src_ref=stats.at[other], dst_ref=stats.at[other], send_sem=s_send.at[o], recv_sem=s_recv.at[other],
            device_id=peer(o), device_id_type=MESH).wait_recv()

    each_peer(lambda o: stat_copy(o).start())
    each_peer(stat_wait)

    whole = jnp.sum(jnp.sum(stats[...], axis=0), axis=1, keepdims=True)
    whole = jnp.broadcast_to(whole, (8, coef.shape[1]))
    grad_norm, image_norm, cross, change_norm = (whole[i:i + 1] for i in range(4))
    step_size = grad_norm / image_norm
    new_norm = grad_norm + step_size * (step_size * change_norm - 2.0 * cross)
    ratio = new_norm / grad_norm
    coef[...] = jnp.concatenate([step_size, ratio] * 4, axis=0)

    def sent(when, *copies):
        @pl.when(when)
        def _():
            for copy in copies:
                copy.wait_send()

    sent(later, *d_step)
    sent(earlier, *r_step, *a_step)
    sent(upper, d_up, r_up, a_up)
    sent(lower, d_down, r_down, a_down)
    each_peer(lambda o: stat_copy(o).wait_send())


def finish(x, r, d, a, g, w, coef, x_out, r_out, d_out, xs, rs, ds, sem):
    step_size, ratio = coef[0:1], coef[1:2]
    writes = []
    for k in range(x.shape[0]):
        xs[k] = x[k] + step_size * d[k]
        rs[k] = r[k] - step_size * a[k]
        ds[k] = g[k] - step_size * w[k] + ratio * d[k]
        for i, (src, dst) in enumerate(((xs, x_out), (rs, r_out), (ds, d_out))):
            write = pltpu.make_async_copy(src.at[k], dst.at[k], sem.at[i, k])
            write.start()
            writes.append(write)
    for write in writes:
        write.wait()


def local(T, S, solution, residual, direction, capacity):
    L, X, Y = capacity.shape
    field = jax.ShapeDtypeStruct((L, X, Y), jnp.float32)
    whole = pltpu.VMEM((L, X, Y), jnp.float32)
    halo = pltpu.VMEM((2, X, Y), jnp.float32)
    near, far = pl.BlockSpec(memory_space=pltpu.VMEM), pl.BlockSpec(memory_space=pltpu.HBM)
    kept = pl.pallas_call(
        functools.partial(exchange, T, S),
        out_shape=(field,) * 6 + (jax.ShapeDtypeStruct((8, Y), jnp.float32),),
        in_specs=[far] * 4,
        out_specs=(near,) * 7,
        scratch_shapes=[whole] * 4 + [halo] * 3 + [
            pltpu.VMEM((T * S, 8, Y), jnp.float32),
            pltpu.SemaphoreType.DMA((4,)),
            pltpu.SemaphoreType.DMA((3, L)),
            pltpu.SemaphoreType.DMA((3, L)),
            pltpu.SemaphoreType.DMA((3, 2)),
            pltpu.SemaphoreType.DMA((3, 2)),
            pltpu.SemaphoreType.DMA((T * S,)),
            pltpu.SemaphoreType.DMA((T * S,)),
        ],
        compiler_params=pltpu.CompilerParams(
            collective_id=0, has_side_effects=True, vmem_limit_bytes=53568 * 1024),
    )(solution[0], residual[0], direction[0], capacity)
    outs = pl.pallas_call(
        finish,
        out_shape=(field,) * 3,
        in_specs=[near] * 7,
        out_specs=(far,) * 3,
        scratch_shapes=[whole] * 3 + [pltpu.SemaphoreType.DMA((3, L))],
        compiler_params=pltpu.CompilerParams(vmem_limit_bytes=16 * 1024 * 1024),
    )(*kept)
    return tuple(out[None] for out in outs)


def solution(mesh):
    field = P(("groups", "tm"), "space", None, None)
    return jax.shard_map(
        functools.partial(local, mesh.shape["tm"], mesh.shape["space"]),
        mesh=mesh,
        in_specs=(field, field, field, P(("groups", "space"), None, None)),
        out_specs=(field, field, field),
        check_vma=False,
    )
```

```python
import functools

import jax
import jax.numpy as jnp
from jax import lax
from jax.experimental import pallas as pl
from jax.experimental.pallas import tpu as pltpu
from jax.sharding import PartitionSpec as P

MESH = pl.DeviceIdType.MESH


def beside(v, up, down):
    nx, ny = v.shape
    row = lax.broadcasted_iota(jnp.int32, v.shape, 0)
    col = lax.broadcasted_iota(jnp.int32, v.shape, 1)
    total = up + down
    total = total + jnp.where(row == 0, 0.0, pltpu.roll(v, 1, 0))
    total = total + jnp.where(row == nx - 1, 0.0, pltpu.roll(v, nx - 1, 0))
    total = total + jnp.where(col == 0, 0.0, pltpu.roll(v, 1, 1))
    return total + jnp.where(col == ny - 1, 0.0, pltpu.roll(v, ny - 1, 1))


def spatial(ref, halo, capacity, k):
    last = ref.shape[0] - 1
    v = ref[k]
    up = ref[k - 1] if k > 0 else halo[0]
    down = ref[k + 1] if k < last else halo[1]
    return (6.0 + capacity) * v - beside(v, up, down)


def folded(x):
    return jnp.sum(x, axis=0, keepdims=True)


def exchange(
    T, S, x_in, r_in, d_in, c_in, xv, rv, dv, av, gv, wv, coef,
    cv, sv, rn, dp, sn, zr, zd, za, mine, theirs, stats,
    in_sem, t_send, t_recv, z_send, z_recv, s_send, s_recv, gate,
):
    L = rv.shape[0]
    N = T * S
    F = L // 2 - 1
    others = [k for k in range(L) if k != F]
    t, s = lax.axis_index("tm"), lax.axis_index("space")
    me = t * S + s
    earlier, later = t > 0, t < T - 1
    lower, upper = s > 0, s < S - 1
    beyond = ((earlier, {"tm": t - 1}), (later, {"tm": t + 1}), (lower, {"space": s - 1}), (upper, {"space": s + 1}))
    count = sum(jnp.where(when, 1, 0) for when, _ in beyond)

    loads = [
        pltpu.make_async_copy(src, dst, in_sem.at[i])
        for i, (src, dst) in enumerate(((d_in, dv), (c_in, cv), (r_in, rv), (x_in, xv)))
    ]
    for load in loads:
        load.start()

    def greet(sem):
        for when, place in beyond:
            @pl.when(when)
            def _():
                pl.semaphore_signal(sem, inc=1, device_id=place, device_id_type=MESH)

    barrier = pltpu.get_barrier_semaphore()
    greet(barrier)

    @pl.when(jnp.logical_not(earlier))
    def _():
        dp[...] = jnp.zeros_like(dp)

    @pl.when(jnp.logical_not(later))
    def _():
        rn[...] = jnp.zeros_like(rn)
        sn[...] = jnp.zeros_like(sn)

    @pl.when(jnp.logical_not(lower))
    def _():
        for z in (zr, zd, za):
            z[0] = jnp.zeros(z.shape[1:], z.dtype)

    @pl.when(jnp.logical_not(upper))
    def _():
        for z in (zr, zd, za):
            z[1] = jnp.zeros(z.shape[1:], z.dtype)

    pl.semaphore_wait(barrier, count)

    rounds = T + S - 3
    share = -(-rounds // 5)
    done = [0]

    def pass_on():
        for _ in range(min(share, rounds - done[0])):
            greet(gate.at[done[0]])
            pl.semaphore_wait(gate.at[done[0]], count)
            done[0] += 1

    def step_copy(i, src, dst, k, to):
        return pltpu.make_async_remote_copy(
            src_ref=src.at[k], dst_ref=dst.at[k], send_sem=t_send.at[i, k], recv_sem=t_recv.at[i, k],
            device_id={"tm": to}, device_id_type=MESH)

    def layer_copy(i, src, dst, up):
        return pltpu.make_async_remote_copy(
            src_ref=src.at[L - 1 if up else 0], dst_ref=dst.at[0 if up else 1],
            send_sem=z_send.at[i, 0 if up else 1], recv_sem=z_recv.at[i, 0 if up else 1],
            device_id={"space": s + 1 if up else s - 1}, device_id_type=MESH)

    d_step = [step_copy(0, d_in, dp, k, t + 1) for k in range(L)]
    r_step = [step_copy(1, r_in, rn, k, t - 1) for k in range(L)]
    s_step = [step_copy(2, sv, sn, k, t - 1) for k in range(L)]
    f_step = [step_copy(3, mine, theirs, i, t + 1) for i in range(2)]
    d_up, d_down = layer_copy(0, d_in, zd, True), layer_copy(0, d_in, zd, False)
    r_up, r_down = layer_copy(1, r_in, zr, True), layer_copy(1, r_in, zr, False)
    a_up, a_down = layer_copy(2, av, za, True), layer_copy(2, av, za, False)

    def go(when, *copies):
        @pl.when(when)
        def _():
            for copy in copies:
                copy.start()

    def arrive(when, *copies):
        @pl.when(when)
        def _():
            for copy in copies:
                copy.wait_recv()

    go(upper, d_up)
    go(lower, d_down)
    go(later, *d_step)
    go(earlier, *[r_step[k] for k in others])
    go(upper, r_up)
    go(lower, r_down)

    for load in loads:
        load.wait()
    middle = [k for k in range(1, L - 1)]
    for k in middle:
        sv[k] = spatial(dv, zd, cv[k], k)
        if k != F:
            go(earlier, s_step[k])
    arrive(lower, d_up)
    arrive(upper, d_down)
    for k in (0, L - 1):
        sv[k] = spatial(dv, zd, cv[k], k)
        if k != F:
            go(earlier, s_step[k])
    pass_on()
    for k in middle:
        gv[k] = spatial(rv, zr, cv[k], k)
    mine[0] = gv[F]
    go(later, f_step[0])
    arrive(lower, r_up)
    arrive(upper, r_down)
    for k in (0, L - 1):
        gv[k] = spatial(rv, zr, cv[k], k)
    pass_on()

    aa = jnp.zeros((1, cv.shape[2]), jnp.float32)
    for k in range(L):
        arrive(earlier, d_step[k])
        image = sv[k] - cv[k] * dp[k]
        av[k] = image
        aa = aa + folded(image * image)
        if k == 0:
            go(lower, a_down)
        if k == F + 1:
            mine[1] = spatial(av, za, cv[F], F)
            go(later, f_step[1])
        if k == L - 1:
            go(upper, a_up)
        if k < 3:
            pass_on()
    go(earlier, r_step[F], s_step[F])

    gg = jnp.zeros((1, cv.shape[2]), jnp.float32)
    for k in others:
        arrive(later, r_step[k])
        gradient = gv[k] - cv[k] * rn[k]
        gv[k] = gradient
        gg = gg + folded(gradient * gradient)

    has_next = jnp.where(later, 1.0, 0.0)
    gw = jnp.zeros((1, cv.shape[2]), jnp.float32)
    ww = jnp.zeros((1, cv.shape[2]), jnp.float32)
    for k in others:
        if k not in (0, L - 1):
            wv[k] = spatial(av, za, cv[k], k)
    arrive(lower, a_up)
    arrive(upper, a_down)
    for k in (0, L - 1):
        wv[k] = spatial(av, za, cv[k], k)
    for k in others:
        arrive(later, s_step[k])
        change = wv[k] - cv[k] * (has_next * (sn[k] - cv[k] * dv[k]))
        wv[k] = change
        gw = gw + folded(gv[k] * change)
        ww = ww + folded(change * change)

    stats[me] = jnp.concatenate([gg, aa, gw, ww, gg, aa, gw, ww], axis=0)

    def add(gradient, change):
        square = folded(gradient * gradient)
        stats[me] += jnp.concatenate(
            [square, jnp.zeros_like(square), folded(gradient * change), folded(change * change)] * 2, axis=0)

    @pl.when(earlier)
    def _():
        for copy in f_step:
            copy.wait_recv()
        add(theirs[0] - cv[F] * rv[F], theirs[1] - cv[F] * av[F])

    @pl.when(jnp.logical_not(later))
    def _():
        add(mine[0], mine[1])

    def peer(o):
        other = lax.rem(me + o, N)
        return {"tm": lax.div(other, S), "space": lax.rem(other, S)}

    def each_peer(do):
        if N <= 16:
            for o in sorted(range(1, N), key=lambda o: -min(o, N - o)):
                do(o)
        else:
            def body(o, carry):
                do(o)
                return carry
            lax.fori_loop(1, N, body, 0)

    def stat_copy(o):
        return pltpu.make_async_remote_copy(
            src_ref=stats.at[me], dst_ref=stats.at[me], send_sem=s_send.at[o], recv_sem=s_recv.at[me],
            device_id=peer(o), device_id_type=MESH)

    def stat_wait(o):
        other = lax.rem(me + o, N)
        pltpu.make_async_remote_copy(
            src_ref=stats.at[other], dst_ref=stats.at[other], send_sem=s_send.at[o], recv_sem=s_recv.at[other],
            device_id=peer(o), device_id_type=MESH).wait_recv()

    each_peer(lambda o: stat_copy(o).start())

    arrive(later, r_step[F], s_step[F])
    gv[F] = mine[0] - cv[F] * rn[F]
    wv[F] = mine[1] - cv[F] * (has_next * (sn[F] - cv[F] * dv[F]))

    def sent(when, *copies):
        @pl.when(when)
        def _():
            for copy in copies:
                copy.wait_send()

    sent(later, *d_step, *f_step)
    sent(earlier, *r_step, *s_step)
    sent(upper, d_up, r_up, a_up)
    sent(lower, d_down, r_down, a_down)
    each_peer(stat_wait)

    whole = jnp.sum(jnp.sum(stats[...], axis=0), axis=1, keepdims=True)
    whole = jnp.broadcast_to(whole, (8, coef.shape[1]))
    grad_norm, image_norm, cross, change_norm = (whole[i:i + 1] for i in range(4))
    step_size = grad_norm / image_norm
    new_norm = grad_norm + step_size * (step_size * change_norm - 2.0 * cross)
    ratio = new_norm / grad_norm
    coef[...] = jnp.concatenate([step_size, ratio] * 4, axis=0)
    each_peer(lambda o: stat_copy(o).wait_send())


def finish(x, r, d, a, g, w, coef, x_out, r_out, d_out, xs, rs, ds, sem):
    step_size, ratio = coef[0:1], coef[1:2]
    writes = []
    for k in range(x.shape[0]):
        xs[k] = x[k] + step_size * d[k]
        rs[k] = r[k] - step_size * a[k]
        ds[k] = g[k] - step_size * w[k] + ratio * d[k]
        for i, (src, dst) in enumerate(((xs, x_out), (rs, r_out), (ds, d_out))):
            write = pltpu.make_async_copy(src.at[k], dst.at[k], sem.at[i, k])
            write.start()
            writes.append(write)
    for write in writes:
        write.wait()


def local(T, S, solution, residual, direction, capacity):
    L, X, Y = capacity.shape
    field = jax.ShapeDtypeStruct((L, X, Y), jnp.float32)
    whole = pltpu.VMEM((L, X, Y), jnp.float32)
    halo = pltpu.VMEM((2, X, Y), jnp.float32)
    near, far = pl.BlockSpec(memory_space=pltpu.VMEM), pl.BlockSpec(memory_space=pltpu.HBM)
    kept = pl.pallas_call(
        functools.partial(exchange, T, S),
        out_shape=(field,) * 6 + (jax.ShapeDtypeStruct((8, Y), jnp.float32),),
        in_specs=[far] * 4,
        out_specs=(near,) * 7,
        scratch_shapes=[whole] * 5 + [halo] * 5 + [
            pltpu.VMEM((T * S, 8, Y), jnp.float32),
            pltpu.SemaphoreType.DMA((4,)),
            pltpu.SemaphoreType.DMA((4, L)),
            pltpu.SemaphoreType.DMA((4, L)),
            pltpu.SemaphoreType.DMA((3, 2)),
            pltpu.SemaphoreType.DMA((3, 2)),
            pltpu.SemaphoreType.DMA((T * S,)),
            pltpu.SemaphoreType.DMA((T * S,)),
            pltpu.SemaphoreType.REGULAR((T + S - 3,)),
        ],
        compiler_params=pltpu.CompilerParams(
            collective_id=0, has_side_effects=True, vmem_limit_bytes=53568 * 1024),
    )(solution[0], residual[0], direction[0], capacity)
    outs = pl.pallas_call(
        finish,
        out_shape=(field,) * 3,
        in_specs=[near] * 7,
        out_specs=(far,) * 3,
        scratch_shapes=[whole] * 3 + [pltpu.SemaphoreType.DMA((3, L))],
        compiler_params=pltpu.CompilerParams(vmem_limit_bytes=16 * 1024 * 1024),
    )(*kept)
    return tuple(out[None] for out in outs)


def solution(mesh):
    field = P(("groups", "tm"), "space", None, None)
    return jax.shard_map(
        functools.partial(local, mesh.shape["tm"], mesh.shape["space"]),
        mesh=mesh,
        in_specs=(field, field, field, P(("groups", "space"), None, None)),
        out_specs=(field, field, field),
        check_vma=False,
    )
```

```python
import functools

import jax
import jax.numpy as jnp
from jax import lax
from jax.experimental import pallas as pl
from jax.experimental.pallas import tpu as pltpu
from jax.sharding import PartitionSpec as P

MESH = pl.DeviceIdType.MESH


def beside(v, up, down):
    nx, ny = v.shape
    row = lax.broadcasted_iota(jnp.int32, v.shape, 0)
    col = lax.broadcasted_iota(jnp.int32, v.shape, 1)
    total = up + down
    total = total + jnp.where(row == 0, 0.0, pltpu.roll(v, 1, 0))
    total = total + jnp.where(row == nx - 1, 0.0, pltpu.roll(v, nx - 1, 0))
    total = total + jnp.where(col == 0, 0.0, pltpu.roll(v, 1, 1))
    return total + jnp.where(col == ny - 1, 0.0, pltpu.roll(v, ny - 1, 1))


def spatial(ref, halo, capacity, k):
    last = ref.shape[0] - 1
    v = ref[k]
    up = ref[k - 1] if k > 0 else halo[0]
    down = ref[k + 1] if k < last else halo[1]
    return (6.0 + capacity) * v - beside(v, up, down)


def folded(x):
    return jnp.sum(x, axis=0, keepdims=True)


def exchange(
    T, S, x_in, r_in, d_in, c_in, xv, rv, dv, av, gv, wv, coef,
    cv, sv, rn, dp, sn, zr, zd, za, mine, theirs, stats,
    in_sem, t_send, t_recv, z_send, z_recv, s_send, s_recv, gate,
):
    L = rv.shape[0]
    N = T * S
    F = L // 2 - 1
    others = [k for k in range(L) if k != F]
    t, s = lax.axis_index("tm"), lax.axis_index("space")
    me = t * S + s
    earlier, later = t > 0, t < T - 1
    lower, upper = s > 0, s < S - 1
    beyond = ((earlier, {"tm": t - 1}), (later, {"tm": t + 1}), (lower, {"space": s - 1}), (upper, {"space": s + 1}))
    count = sum(jnp.where(when, 1, 0) for when, _ in beyond)

    loads = [
        pltpu.make_async_copy(src, dst, in_sem.at[i])
        for i, (src, dst) in enumerate(((d_in, dv), (c_in, cv), (r_in, rv), (x_in, xv)))
    ]
    for load in loads:
        load.start()

    def greet(sem):
        for when, place in beyond:
            @pl.when(when)
            def _():
                pl.semaphore_signal(sem, inc=1, device_id=place, device_id_type=MESH)

    barrier = pltpu.get_barrier_semaphore()
    greet(barrier)

    @pl.when(jnp.logical_not(earlier))
    def _():
        dp[...] = jnp.zeros_like(dp)

    @pl.when(jnp.logical_not(later))
    def _():
        rn[...] = jnp.zeros_like(rn)
        sn[...] = jnp.zeros_like(sn)

    @pl.when(jnp.logical_not(lower))
    def _():
        for z in (zr, zd, za):
            z[0] = jnp.zeros(z.shape[1:], z.dtype)

    @pl.when(jnp.logical_not(upper))
    def _():
        for z in (zr, zd, za):
            z[1] = jnp.zeros(z.shape[1:], z.dtype)

    pl.semaphore_wait(barrier, count)

    rounds = T + S - 3
    share = -(-(rounds - 1) // 4)
    done = [0]

    def pass_on(limit=rounds):
        for _ in range(min(limit, rounds - done[0])):
            pl.semaphore_wait(gate.at[done[0]], count)
            done[0] += 1
            if done[0] < rounds:
                greet(gate.at[done[0]])

    greet(gate.at[0])

    def step_copy(i, src, dst, k, to):
        return pltpu.make_async_remote_copy(
            src_ref=src.at[k], dst_ref=dst.at[k], send_sem=t_send.at[i, k], recv_sem=t_recv.at[i, k],
            device_id={"tm": to}, device_id_type=MESH)

    def layer_copy(i, src, dst, up):
        return pltpu.make_async_remote_copy(
            src_ref=src.at[L - 1 if up else 0], dst_ref=dst.at[0 if up else 1],
            send_sem=z_send.at[i, 0 if up else 1], recv_sem=z_recv.at[i, 0 if up else 1],
            device_id={"space": s + 1 if up else s - 1}, device_id_type=MESH)

    d_step = [step_copy(0, d_in, dp, k, t + 1) for k in range(L)]
    r_step = [step_copy(1, r_in, rn, k, t - 1) for k in range(L)]
    s_step = [step_copy(2, sv, sn, k, t - 1) for k in range(L)]
    f_step = [step_copy(3, mine, theirs, i, t + 1) for i in range(2)]
    d_up, d_down = layer_copy(0, d_in, zd, True), layer_copy(0, d_in, zd, False)
    r_up, r_down = layer_copy(1, r_in, zr, True), layer_copy(1, r_in, zr, False)
    a_up, a_down = layer_copy(2, av, za, True), layer_copy(2, av, za, False)

    def go(when, *copies):
        @pl.when(when)
        def _():
            for copy in copies:
                copy.start()

    def arrive(when, *copies):
        @pl.when(when)
        def _():
            for copy in copies:
                copy.wait_recv()

    go(upper, d_up)
    go(lower, d_down)
    go(later, *d_step)
    go(earlier, *[r_step[k] for k in others])
    go(upper, r_up)
    go(lower, r_down)

    for load in loads:
        load.wait()
    middle = [k for k in range(1, L - 1)]
    for k in middle:
        sv[k] = spatial(dv, zd, cv[k], k)
        if k != F:
            go(earlier, s_step[k])
    arrive(lower, d_up)
    arrive(upper, d_down)
    for k in (0, L - 1):
        sv[k] = spatial(dv, zd, cv[k], k)
        if k != F:
            go(earlier, s_step[k])
    pass_on(share)
    for k in middle:
        gv[k] = spatial(rv, zr, cv[k], k)
    mine[0] = gv[F]
    go(later, f_step[0])
    arrive(lower, r_up)
    arrive(upper, r_down)
    for k in (0, L - 1):
        gv[k] = spatial(rv, zr, cv[k], k)
    pass_on(share)

    aa = jnp.zeros((1, cv.shape[2]), jnp.float32)
    for k in range(L):
        arrive(earlier, d_step[k])
        image = sv[k] - cv[k] * dp[k]
        av[k] = image
        aa = aa + folded(image * image)
        if k == 0:
            go(lower, a_down)
        if k == F + 1:
            mine[1] = spatial(av, za, cv[F], F)
            go(later, f_step[1])
        if k == L - 1:
            go(upper, a_up)
        if k < 2:
            pass_on(share)
    go(earlier, r_step[F])

    gg = jnp.zeros((1, cv.shape[2]), jnp.float32)
    for k in others:
        arrive(later, r_step[k])
        gradient = gv[k] - cv[k] * rn[k]
        gv[k] = gradient
        gg = gg + folded(gradient * gradient)

    has_next = jnp.where(later, 1.0, 0.0)
    gw = jnp.zeros((1, cv.shape[2]), jnp.float32)
    ww = jnp.zeros((1, cv.shape[2]), jnp.float32)
    for k in others:
        if k not in (0, L - 1):
            wv[k] = spatial(av, za, cv[k], k)
    arrive(lower, a_up)
    arrive(upper, a_down)
    for k in (0, L - 1):
        wv[k] = spatial(av, za, cv[k], k)
    for k in others:
        arrive(later, s_step[k])
        change = wv[k] - cv[k] * (has_next * (sn[k] - cv[k] * dv[k]))
        wv[k] = change
        gw = gw + folded(gv[k] * change)
        ww = ww + folded(change * change)

    stats[me] = jnp.concatenate([gg, aa, gw, ww, gg, aa, gw, ww], axis=0)

    def add(gradient, change):
        square = folded(gradient * gradient)
        stats[me] += jnp.concatenate(
            [square, jnp.zeros_like(square), folded(gradient * change), folded(change * change)] * 2, axis=0)

    @pl.when(earlier)
    def _():
        for copy in f_step:
            copy.wait_recv()
        add(theirs[0] - cv[F] * rv[F], theirs[1] - cv[F] * av[F])

    @pl.when(jnp.logical_not(later))
    def _():
        add(mine[0], mine[1])

    def peer(o):
        other = lax.rem(me + o, N)
        return {"tm": lax.div(other, S), "space": lax.rem(other, S)}

    def each_peer(do):
        if N <= 16:
            for o in sorted(range(1, N), key=lambda o: -min(o, N - o)):
                do(o)
        else:
            def body(o, carry):
                do(o)
                return carry
            lax.fori_loop(1, N, body, 0)

    def stat_copy(o):
        return pltpu.make_async_remote_copy(
            src_ref=stats.at[me], dst_ref=stats.at[me], send_sem=s_send.at[o], recv_sem=s_recv.at[me],
            device_id=peer(o), device_id_type=MESH)

    def stat_wait(o):
        other = lax.rem(me + o, N)
        pltpu.make_async_remote_copy(
            src_ref=stats.at[other], dst_ref=stats.at[other], send_sem=s_send.at[o], recv_sem=s_recv.at[other],
            device_id=peer(o), device_id_type=MESH).wait_recv()

    pass_on()
    each_peer(lambda o: stat_copy(o).start())
    go(earlier, s_step[F])

    arrive(later, r_step[F], s_step[F])
    gv[F] = mine[0] - cv[F] * rn[F]
    wv[F] = mine[1] - cv[F] * (has_next * (sn[F] - cv[F] * dv[F]))

    def sent(when, *copies):
        @pl.when(when)
        def _():
            for copy in copies:
                copy.wait_send()

    sent(later, *d_step, *f_step)
    sent(earlier, *r_step, *s_step)
    sent(upper, d_up, r_up, a_up)
    sent(lower, d_down, r_down, a_down)
    each_peer(stat_wait)

    whole = jnp.sum(jnp.sum(stats[...], axis=0), axis=1, keepdims=True)
    whole = jnp.broadcast_to(whole, (8, coef.shape[1]))
    grad_norm, image_norm, cross, change_norm = (whole[i:i + 1] for i in range(4))
    step_size = grad_norm / image_norm
    new_norm = grad_norm + step_size * (step_size * change_norm - 2.0 * cross)
    ratio = new_norm / grad_norm
    coef[...] = jnp.concatenate([step_size, ratio] * 4, axis=0)
    each_peer(lambda o: stat_copy(o).wait_send())


def finish(x, r, d, a, g, w, coef, x_out, r_out, d_out, xs, rs, ds, sem):
    step_size, ratio = coef[0:1], coef[1:2]
    writes = []
    for k in range(x.shape[0]):
        xs[k] = x[k] + step_size * d[k]
        rs[k] = r[k] - step_size * a[k]
        ds[k] = g[k] - step_size * w[k] + ratio * d[k]
        for i, (src, dst) in enumerate(((xs, x_out), (rs, r_out), (ds, d_out))):
            write = pltpu.make_async_copy(src.at[k], dst.at[k], sem.at[i, k])
            write.start()
            writes.append(write)
    for write in writes:
        write.wait()


def local(T, S, solution, residual, direction, capacity):
    L, X, Y = capacity.shape
    field = jax.ShapeDtypeStruct((L, X, Y), jnp.float32)
    whole = pltpu.VMEM((L, X, Y), jnp.float32)
    halo = pltpu.VMEM((2, X, Y), jnp.float32)
    near, far = pl.BlockSpec(memory_space=pltpu.VMEM), pl.BlockSpec(memory_space=pltpu.HBM)
    kept = pl.pallas_call(
        functools.partial(exchange, T, S),
        out_shape=(field,) * 6 + (jax.ShapeDtypeStruct((8, Y), jnp.float32),),
        in_specs=[far] * 4,
        out_specs=(near,) * 7,
        scratch_shapes=[whole] * 5 + [halo] * 5 + [
            pltpu.VMEM((T * S, 8, Y), jnp.float32),
            pltpu.SemaphoreType.DMA((4,)),
            pltpu.SemaphoreType.DMA((4, L)),
            pltpu.SemaphoreType.DMA((4, L)),
            pltpu.SemaphoreType.DMA((3, 2)),
            pltpu.SemaphoreType.DMA((3, 2)),
            pltpu.SemaphoreType.DMA((T * S,)),
            pltpu.SemaphoreType.DMA((T * S,)),
            pltpu.SemaphoreType.REGULAR((T + S - 3,)),
        ],
        compiler_params=pltpu.CompilerParams(
            collective_id=0, has_side_effects=True, vmem_limit_bytes=53568 * 1024),
    )(solution[0], residual[0], direction[0], capacity)
    outs = pl.pallas_call(
        finish,
        out_shape=(field,) * 3,
        in_specs=[near] * 7,
        out_specs=(far,) * 3,
        scratch_shapes=[whole] * 3 + [pltpu.SemaphoreType.DMA((3, L))],
        compiler_params=pltpu.CompilerParams(vmem_limit_bytes=16 * 1024 * 1024),
    )(*kept)
    return tuple(out[None] for out in outs)


def solution(mesh):
    field = P(("groups", "tm"), "space", None, None)
    return jax.shard_map(
        functools.partial(local, mesh.shape["tm"], mesh.shape["space"]),
        mesh=mesh,
        in_specs=(field, field, field, P(("groups", "space"), None, None)),
        out_specs=(field, field, field),
        check_vma=False,
    )
```

```python
import functools

import jax
import jax.numpy as jnp
from jax import lax
from jax.experimental import pallas as pl
from jax.experimental.pallas import tpu as pltpu
from jax.sharding import PartitionSpec as P

MESH = pl.DeviceIdType.MESH


def beside(v, up, down):
    nx, ny = v.shape
    row = lax.broadcasted_iota(jnp.int32, v.shape, 0)
    col = lax.broadcasted_iota(jnp.int32, v.shape, 1)
    total = up + down
    total = total + jnp.where(row == 0, 0.0, pltpu.roll(v, 1, 0))
    total = total + jnp.where(row == nx - 1, 0.0, pltpu.roll(v, nx - 1, 0))
    total = total + jnp.where(col == 0, 0.0, pltpu.roll(v, 1, 1))
    return total + jnp.where(col == ny - 1, 0.0, pltpu.roll(v, ny - 1, 1))


def spatial(ref, halo, capacity, k):
    last = ref.shape[0] - 1
    v = ref[k]
    up = ref[k - 1] if k > 0 else halo[0]
    down = ref[k + 1] if k < last else halo[1]
    return (6.0 + capacity) * v - beside(v, up, down)


def folded(x):
    return jnp.sum(x, axis=0, keepdims=True)


def exchange(
    T, S, x_in, r_in, d_in, c_in, xv, rv, dv, av, gv, wv, coef,
    cv, sv, rn, dp, sn, zr, zd, za, mine, theirs, stats,
    in_sem, t_send, t_recv, z_send, z_recv, s_send, s_recv, gate,
):
    L = rv.shape[0]
    N = T * S
    F = L // 2 - 1
    others = [k for k in range(L) if k != F]
    t, s = lax.axis_index("tm"), lax.axis_index("space")
    me = t * S + s
    earlier, later = t > 0, t < T - 1
    lower, upper = s > 0, s < S - 1
    beyond = ((earlier, {"tm": t - 1}), (later, {"tm": t + 1}), (lower, {"space": s - 1}), (upper, {"space": s + 1}))
    count = sum(jnp.where(when, 1, 0) for when, _ in beyond)

    loads = [
        pltpu.make_async_copy(src, dst, in_sem.at[i])
        for i, (src, dst) in enumerate(((d_in, dv), (c_in, cv), (r_in, rv), (x_in, xv)))
    ]
    for load in loads:
        load.start()

    def greet(sem):
        for when, place in beyond:
            @pl.when(when)
            def _():
                pl.semaphore_signal(sem, inc=1, device_id=place, device_id_type=MESH)

    def turned(i, by, n):
        return jnp.where(i + by >= n, i + by - n, i + by)

    def shift(o):
        if isinstance(o, int):
            return turned(t, o // S, T), turned(s, o % S, S)
        return turned(t, lax.div(o, S), T), turned(s, lax.rem(o, S), S)

    known = {o: shift(o) for o in range(1, N)} if N <= 16 else {}

    def place_of(o):
        return known[o] if isinstance(o, int) else shift(o)

    def peer(o):
        other_t, other_s = place_of(o)
        return {"tm": other_t, "space": other_s}

    barrier = pltpu.get_barrier_semaphore()
    greet(barrier)

    @pl.when(jnp.logical_not(earlier))
    def _():
        dp[...] = jnp.zeros_like(dp)

    @pl.when(jnp.logical_not(later))
    def _():
        rn[...] = jnp.zeros_like(rn)
        sn[...] = jnp.zeros_like(sn)

    @pl.when(jnp.logical_not(lower))
    def _():
        for z in (zr, zd, za):
            z[0] = jnp.zeros(z.shape[1:], z.dtype)

    @pl.when(jnp.logical_not(upper))
    def _():
        for z in (zr, zd, za):
            z[1] = jnp.zeros(z.shape[1:], z.dtype)

    pl.semaphore_wait(barrier, count)

    rounds = T + S - 3
    share = -(-(rounds - 1) // 4)
    done = [0]

    def pass_on(limit=rounds):
        for _ in range(min(limit, rounds - done[0])):
            pl.semaphore_wait(gate.at[done[0]], count)
            done[0] += 1
            if done[0] < rounds:
                greet(gate.at[done[0]])

    greet(gate.at[0])

    def step_copy(i, src, dst, k, to):
        return pltpu.make_async_remote_copy(
            src_ref=src.at[k], dst_ref=dst.at[k], send_sem=t_send.at[i, k], recv_sem=t_recv.at[i, k],
            device_id={"tm": to}, device_id_type=MESH)

    def layer_copy(i, src, dst, up):
        return pltpu.make_async_remote_copy(
            src_ref=src.at[L - 1 if up else 0], dst_ref=dst.at[0 if up else 1],
            send_sem=z_send.at[i, 0 if up else 1], recv_sem=z_recv.at[i, 0 if up else 1],
            device_id={"space": s + 1 if up else s - 1}, device_id_type=MESH)

    d_step = [step_copy(0, d_in, dp, k, t + 1) for k in range(L)]
    r_step = [step_copy(1, r_in, rn, k, t - 1) for k in range(L)]
    s_step = [step_copy(2, sv, sn, k, t - 1) for k in range(L)]
    f_step = [step_copy(3, mine, theirs, i, t + 1) for i in range(2)]
    d_up, d_down = layer_copy(0, d_in, zd, True), layer_copy(0, d_in, zd, False)
    r_up, r_down = layer_copy(1, r_in, zr, True), layer_copy(1, r_in, zr, False)
    a_up, a_down = layer_copy(2, av, za, True), layer_copy(2, av, za, False)

    def go(when, *copies):
        @pl.when(when)
        def _():
            for copy in copies:
                copy.start()

    def arrive(when, *copies):
        @pl.when(when)
        def _():
            for copy in copies:
                copy.wait_recv()

    go(upper, d_up)
    go(lower, d_down)
    go(upper, r_up)
    go(lower, r_down)
    go(later, *d_step)
    go(earlier, *[r_step[k] for k in others])

    for load in loads:
        load.wait()
    middle = [k for k in range(1, L - 1)]
    for k in middle:
        sv[k] = spatial(dv, zd, cv[k], k)
        if k != F:
            go(earlier, s_step[k])
    arrive(lower, d_up)
    arrive(upper, d_down)
    for k in (0, L - 1):
        sv[k] = spatial(dv, zd, cv[k], k)
        if k != F:
            go(earlier, s_step[k])
    pass_on(share)
    for k in middle:
        gv[k] = spatial(rv, zr, cv[k], k)
    mine[0] = gv[F]
    go(later, f_step[0])
    arrive(lower, r_up)
    arrive(upper, r_down)
    for k in (0, L - 1):
        gv[k] = spatial(rv, zr, cv[k], k)
    pass_on(share)

    aa = jnp.zeros((1, cv.shape[2]), jnp.float32)
    for k in range(L):
        arrive(earlier, d_step[k])
        image = sv[k] - cv[k] * dp[k]
        av[k] = image
        aa = aa + folded(image * image)
        if k == 0:
            go(lower, a_down)
        if k == F + 1:
            mine[1] = spatial(av, za, cv[F], F)
            go(later, f_step[1])
        if k == L - 1:
            go(upper, a_up)
        if k < 2:
            pass_on(share)
    go(earlier, r_step[F])

    gg = jnp.zeros((1, cv.shape[2]), jnp.float32)
    for k in others:
        arrive(later, r_step[k])
        gradient = gv[k] - cv[k] * rn[k]
        gv[k] = gradient
        gg = gg + folded(gradient * gradient)

    has_next = jnp.where(later, 1.0, 0.0)
    gw = jnp.zeros((1, cv.shape[2]), jnp.float32)
    ww = jnp.zeros((1, cv.shape[2]), jnp.float32)
    nothing = jnp.zeros(cv.shape[1:], jnp.float32)
    wv[0] = (6.0 + cv[0]) * av[0] - beside(av[0], nothing, av[1])
    for k in others:
        if k not in (0, L - 1):
            wv[k] = spatial(av, za, cv[k], k)
    arrive(upper, a_down)
    wv[L - 1] = spatial(av, za, cv[L - 1], L - 1)
    for k in others[1:] + others[:1]:
        arrive(later, s_step[k])
        change = wv[k] - cv[k] * (has_next * (sn[k] - cv[k] * dv[k]))
        if k == 0:
            arrive(lower, a_up)
            change = change - za[0]
        wv[k] = change
        gw = gw + folded(gv[k] * change)
        ww = ww + folded(change * change)

    stats[me] = jnp.concatenate([gg, aa, gw, ww], axis=0)

    def add(gradient, change):
        square = folded(gradient * gradient)
        stats[me] += jnp.concatenate(
            [square, jnp.zeros_like(square), folded(gradient * change), folded(change * change)], axis=0)

    @pl.when(earlier)
    def _():
        for copy in f_step:
            copy.wait_recv()
        add(theirs[0] - cv[F] * rv[F], theirs[1] - cv[F] * av[F])

    @pl.when(jnp.logical_not(later))
    def _():
        add(mine[0], mine[1])

    def each_peer(do):
        if N <= 16:
            for o in sorted(range(1, N), key=lambda o: -min(o, N - o)):
                do(o)
        else:
            def body(o, carry):
                do(o)
                return carry
            lax.fori_loop(1, N, body, 0)

    def stat_copy(o):
        return pltpu.make_async_remote_copy(
            src_ref=stats.at[me], dst_ref=stats.at[me], send_sem=s_send.at[o], recv_sem=s_recv.at[me],
            device_id=peer(o), device_id_type=MESH)

    def stat_wait(o):
        other_t, other_s = place_of(o)
        other = other_t * S + other_s
        pltpu.make_async_remote_copy(
            src_ref=stats.at[other], dst_ref=stats.at[other], send_sem=s_send.at[o], recv_sem=s_recv.at[other],
            device_id=peer(o), device_id_type=MESH).wait_recv()

    pass_on()
    each_peer(lambda o: stat_copy(o).start())
    go(earlier, s_step[F])

    arrive(later, r_step[F], s_step[F])
    gv[F] = mine[0] - cv[F] * rn[F]
    wv[F] = mine[1] - cv[F] * (has_next * (sn[F] - cv[F] * dv[F]))

    def sent(when, *copies):
        @pl.when(when)
        def _():
            for copy in copies:
                copy.wait_send()

    sent(later, *d_step, *f_step)
    sent(earlier, *r_step, *s_step)
    sent(upper, d_up, r_up, a_up)
    sent(lower, d_down, r_down, a_down)
    each_peer(stat_wait)

    whole = jnp.sum(jnp.sum(stats[...], axis=0), axis=1, keepdims=True)
    whole = jnp.broadcast_to(whole, (4, coef.shape[1]))
    grad_norm, image_norm, cross, change_norm = (whole[i:i + 1] for i in range(4))
    step_size = grad_norm / image_norm
    new_norm = grad_norm + step_size * (step_size * change_norm - 2.0 * cross)
    ratio = new_norm / grad_norm
    coef[...] = jnp.concatenate([step_size, ratio] * 4, axis=0)
    each_peer(lambda o: stat_copy(o).wait_send())


def finish(x, r, d, a, g, w, coef, x_out, r_out, d_out, xs, rs, ds, sem):
    step_size, ratio = coef[0:1], coef[1:2]
    writes = []
    for k in range(x.shape[0]):
        xs[k] = x[k] + step_size * d[k]
        rs[k] = r[k] - step_size * a[k]
        ds[k] = g[k] - step_size * w[k] + ratio * d[k]
        for i, (src, dst) in enumerate(((xs, x_out), (rs, r_out), (ds, d_out))):
            write = pltpu.make_async_copy(src.at[k], dst.at[k], sem.at[i, k])
            write.start()
            writes.append(write)
    for write in writes:
        write.wait()


def local(T, S, solution, residual, direction, capacity):
    L, X, Y = capacity.shape
    field = jax.ShapeDtypeStruct((L, X, Y), jnp.float32)
    whole = pltpu.VMEM((L, X, Y), jnp.float32)
    halo = pltpu.VMEM((2, X, Y), jnp.float32)
    near, far = pl.BlockSpec(memory_space=pltpu.VMEM), pl.BlockSpec(memory_space=pltpu.HBM)
    kept = pl.pallas_call(
        functools.partial(exchange, T, S),
        out_shape=(field,) * 6 + (jax.ShapeDtypeStruct((8, Y), jnp.float32),),
        in_specs=[far] * 4,
        out_specs=(near,) * 7,
        scratch_shapes=[whole] * 5 + [halo] * 5 + [
            pltpu.VMEM((T * S, 4, Y), jnp.float32),
            pltpu.SemaphoreType.DMA((4,)),
            pltpu.SemaphoreType.DMA((4, L)),
            pltpu.SemaphoreType.DMA((4, L)),
            pltpu.SemaphoreType.DMA((3, 2)),
            pltpu.SemaphoreType.DMA((3, 2)),
            pltpu.SemaphoreType.DMA((T * S,)),
            pltpu.SemaphoreType.DMA((T * S,)),
            pltpu.SemaphoreType.REGULAR((T + S - 3,)),
        ],
        compiler_params=pltpu.CompilerParams(
            collective_id=0, has_side_effects=True, vmem_limit_bytes=53568 * 1024),
    )(solution[0], residual[0], direction[0], capacity)
    outs = pl.pallas_call(
        finish,
        out_shape=(field,) * 3,
        in_specs=[near] * 7,
        out_specs=(far,) * 3,
        scratch_shapes=[whole] * 3 + [pltpu.SemaphoreType.DMA((3, L))],
        compiler_params=pltpu.CompilerParams(vmem_limit_bytes=16 * 1024 * 1024),
    )(*kept)
    return tuple(out[None] for out in outs)


def solution(mesh):
    field = P(("groups", "tm"), "space", None, None)
    return jax.shard_map(
        functools.partial(local, mesh.shape["tm"], mesh.shape["space"]),
        mesh=mesh,
        in_specs=(field, field, field, P(("groups", "space"), None, None)),
        out_specs=(field, field, field),
        check_vma=False,
    )
```

```python
import functools

import jax
import jax.numpy as jnp
from jax import lax
from jax.experimental import pallas as pl
from jax.experimental.pallas import tpu as pltpu
from jax.sharding import PartitionSpec as P

MESH = pl.DeviceIdType.MESH


def beside(v, up, down):
    nx, ny = v.shape
    row = lax.broadcasted_iota(jnp.int32, v.shape, 0)
    col = lax.broadcasted_iota(jnp.int32, v.shape, 1)
    total = up + down
    total = total + jnp.where(row == 0, 0.0, pltpu.roll(v, 1, 0))
    total = total + jnp.where(row == nx - 1, 0.0, pltpu.roll(v, nx - 1, 0))
    total = total + jnp.where(col == 0, 0.0, pltpu.roll(v, 1, 1))
    return total + jnp.where(col == ny - 1, 0.0, pltpu.roll(v, ny - 1, 1))


def spatial(ref, halo, capacity, k):
    last = ref.shape[0] - 1
    v = ref[k]
    up = ref[k - 1] if k > 0 else halo[0]
    down = ref[k + 1] if k < last else halo[1]
    return (6.0 + capacity) * v - beside(v, up, down)


def folded(x):
    return jnp.sum(x, axis=0, keepdims=True)


def exchange(
    T, S, x_in, r_in, d_in, c_in, xv, rv, dv, av, gv, wv, coef,
    cv, sv, rn, dp, sn, zr, zd, za, mine, theirs, stats,
    in_sem, t_send, t_recv, z_send, z_recv, s_send, s_recv, gate,
):
    L = rv.shape[0]
    N = T * S
    F = L // 2 - 1
    others = [k for k in range(L) if k != F]
    t, s = lax.axis_index("tm"), lax.axis_index("space")
    me = t * S + s
    earlier, later = t > 0, t < T - 1
    lower, upper = s > 0, s < S - 1
    beyond = ((earlier, {"tm": t - 1}), (later, {"tm": t + 1}), (lower, {"space": s - 1}), (upper, {"space": s + 1}))
    count = sum(jnp.where(when, 1, 0) for when, _ in beyond)

    loads = [
        pltpu.make_async_copy(src, dst, in_sem.at[i])
        for i, (src, dst) in enumerate(((d_in, dv), (c_in, cv), (r_in, rv), (x_in, xv)))
    ]
    for load in loads:
        load.start()

    def greet(sem):
        for when, place in beyond:
            @pl.when(when)
            def _():
                pl.semaphore_signal(sem, inc=1, device_id=place, device_id_type=MESH)

    def turned(i, by, n):
        return jnp.where(i + by >= n, i + by - n, i + by)

    def shift(o):
        if isinstance(o, int):
            return turned(t, o // S, T), turned(s, o % S, S)
        return turned(t, lax.div(o, S), T), turned(s, lax.rem(o, S), S)

    known = {o: shift(o) for o in range(1, N)} if N <= 16 else {}

    def place_of(o):
        return known[o] if isinstance(o, int) else shift(o)

    def peer(o):
        other_t, other_s = place_of(o)
        return {"tm": other_t, "space": other_s}

    barrier = pltpu.get_barrier_semaphore()
    greet(barrier)

    @pl.when(jnp.logical_not(earlier))
    def _():
        dp[...] = jnp.zeros_like(dp)

    @pl.when(jnp.logical_not(later))
    def _():
        rn[...] = jnp.zeros_like(rn)
        sn[...] = jnp.zeros_like(sn)

    @pl.when(jnp.logical_not(lower))
    def _():
        for z in (zr, zd, za):
            z[0] = jnp.zeros(z.shape[1:], z.dtype)

    @pl.when(jnp.logical_not(upper))
    def _():
        for z in (zr, zd, za):
            z[1] = jnp.zeros(z.shape[1:], z.dtype)

    pl.semaphore_wait(barrier, count)

    rounds = T + S - 3
    share = -(-(rounds - 1) // 4)
    done = [0]

    def pass_on(limit=rounds):
        for _ in range(min(limit, rounds - done[0])):
            pl.semaphore_wait(gate.at[done[0]], count)
            done[0] += 1
            if done[0] < rounds:
                greet(gate.at[done[0]])

    greet(gate.at[0])

    def step_copy(i, src, dst, k, to):
        return pltpu.make_async_remote_copy(
            src_ref=src.at[k], dst_ref=dst.at[k], send_sem=t_send.at[i, k], recv_sem=t_recv.at[i, k],
            device_id={"tm": to}, device_id_type=MESH)

    def layer_copy(i, src, dst, up):
        return pltpu.make_async_remote_copy(
            src_ref=src.at[L - 1 if up else 0], dst_ref=dst.at[0 if up else 1],
            send_sem=z_send.at[i, 0 if up else 1], recv_sem=z_recv.at[i, 0 if up else 1],
            device_id={"space": s + 1 if up else s - 1}, device_id_type=MESH)

    d_step = [step_copy(0, d_in, dp, k, t + 1) for k in range(L)]
    r_step = [step_copy(1, r_in, rn, k, t - 1) for k in range(L)]
    s_step = [step_copy(2, sv, sn, k, t - 1) for k in range(L)]
    f_step = [step_copy(3, mine, theirs, i, t + 1) for i in range(2)]
    d_up, d_down = layer_copy(0, d_in, zd, True), layer_copy(0, d_in, zd, False)
    r_up, r_down = layer_copy(1, r_in, zr, True), layer_copy(1, r_in, zr, False)
    a_up, a_down = layer_copy(2, av, za, True), layer_copy(2, av, za, False)

    def go(when, *copies):
        @pl.when(when)
        def _():
            for copy in copies:
                copy.start()

    def arrive(when, *copies):
        @pl.when(when)
        def _():
            for copy in copies:
                copy.wait_recv()

    go(upper, d_up)
    go(lower, d_down)
    go(upper, r_up)
    go(lower, r_down)
    go(later, *d_step)
    go(earlier, *[r_step[k] for k in others])

    for load in loads:
        load.wait()
    middle = [k for k in range(1, L - 1)]
    for k in middle:
        sv[k] = spatial(dv, zd, cv[k], k)
        if k != F:
            go(earlier, s_step[k])
    arrive(lower, d_up)
    arrive(upper, d_down)
    for k in (0, L - 1):
        sv[k] = spatial(dv, zd, cv[k], k)
        if k != F:
            go(earlier, s_step[k])
    pass_on(share)
    for k in middle:
        gv[k] = spatial(rv, zr, cv[k], k)
    mine[0] = gv[F]
    go(later, f_step[0])
    arrive(lower, r_up)
    arrive(upper, r_down)
    for k in (0, L - 1):
        gv[k] = spatial(rv, zr, cv[k], k)
    pass_on(share)

    aa = jnp.zeros((1, cv.shape[2]), jnp.float32)
    for k in range(L):
        arrive(earlier, d_step[k])
        image = sv[k] - cv[k] * dp[k]
        av[k] = image
        aa = aa + folded(image * image)
        if k == 0:
            go(lower, a_down)
        if k == F + 1:
            mine[1] = spatial(av, za, cv[F], F)
            go(later, f_step[1])
        if k == L - 1:
            go(upper, a_up)
        if k < 2:
            pass_on(share)
    go(earlier, r_step[F])

    gg = jnp.zeros((1, cv.shape[2]), jnp.float32)
    for k in others:
        arrive(later, r_step[k])
        gradient = gv[k] - cv[k] * rn[k]
        gv[k] = gradient
        gg = gg + folded(gradient * gradient)

    has_next = jnp.where(later, 1.0, 0.0)
    gw = jnp.zeros((1, cv.shape[2]), jnp.float32)
    ww = jnp.zeros((1, cv.shape[2]), jnp.float32)
    nothing = jnp.zeros(cv.shape[1:], jnp.float32)
    wv[0] = (6.0 + cv[0]) * av[0] - beside(av[0], nothing, av[1])
    for k in others:
        if k not in (0, L - 1):
            wv[k] = spatial(av, za, cv[k], k)
    arrive(upper, a_down)
    wv[L - 1] = spatial(av, za, cv[L - 1], L - 1)
    def add(gradient, change):
        square = folded(gradient * gradient)
        stats[me] += jnp.concatenate(
            [square, jnp.zeros_like(square), folded(gradient * change), folded(change * change)], axis=0)

    for k in others[1:] + others[:1]:
        arrive(later, s_step[k])
        if k == 0:
            stats[me] = jnp.concatenate([gg, aa, gw, ww], axis=0)

            @pl.when(earlier)
            def _():
                for copy in f_step:
                    copy.wait_recv()
                add(theirs[0] - cv[F] * rv[F], theirs[1] - cv[F] * av[F])

            @pl.when(jnp.logical_not(later))
            def _():
                add(mine[0], mine[1])

            gw, ww = jnp.zeros_like(gw), jnp.zeros_like(ww)
        change = wv[k] - cv[k] * (has_next * (sn[k] - cv[k] * dv[k]))
        if k == 0:
            arrive(lower, a_up)
            change = change - za[0]
        wv[k] = change
        gw = gw + folded(gv[k] * change)
        ww = ww + folded(change * change)

    nil = jnp.zeros_like(gw)
    stats[me] += jnp.concatenate([nil, nil, gw, ww], axis=0)

    def each_peer(do):
        if N <= 16:
            for o in sorted(range(1, N), key=lambda o: -min(o, N - o)):
                do(o)
        else:
            def body(o, carry):
                do(o)
                return carry
            lax.fori_loop(1, N, body, 0)

    def stat_copy(o):
        return pltpu.make_async_remote_copy(
            src_ref=stats.at[me], dst_ref=stats.at[me], send_sem=s_send.at[o], recv_sem=s_recv.at[me],
            device_id=peer(o), device_id_type=MESH)

    def stat_wait(o):
        other_t, other_s = place_of(o)
        other = other_t * S + other_s
        pltpu.make_async_remote_copy(
            src_ref=stats.at[other], dst_ref=stats.at[other], send_sem=s_send.at[o], recv_sem=s_recv.at[other],
            device_id=peer(o), device_id_type=MESH).wait_recv()

    pass_on()
    each_peer(lambda o: stat_copy(o).start())
    go(earlier, s_step[F])

    arrive(later, r_step[F], s_step[F])
    gv[F] = mine[0] - cv[F] * rn[F]
    wv[F] = mine[1] - cv[F] * (has_next * (sn[F] - cv[F] * dv[F]))

    def sent(when, *copies):
        @pl.when(when)
        def _():
            for copy in copies:
                copy.wait_send()

    sent(later, *d_step, *f_step)
    sent(earlier, *r_step, *s_step)
    sent(upper, d_up, r_up, a_up)
    sent(lower, d_down, r_down, a_down)
    each_peer(stat_wait)

    whole = jnp.sum(jnp.sum(stats[...], axis=0), axis=1, keepdims=True)
    whole = jnp.broadcast_to(whole, (4, coef.shape[1]))
    grad_norm, image_norm, cross, change_norm = (whole[i:i + 1] for i in range(4))
    step_size = grad_norm / image_norm
    new_norm = grad_norm + step_size * (step_size * change_norm - 2.0 * cross)
    ratio = new_norm / grad_norm
    coef[...] = jnp.concatenate([step_size, ratio] * 4, axis=0)
    each_peer(lambda o: stat_copy(o).wait_send())


def finish(x, r, d, a, g, w, coef, x_out, r_out, d_out, xs, rs, ds, sem):
    step_size, ratio = coef[0:1], coef[1:2]
    writes = []
    for k in range(x.shape[0]):
        xs[k] = x[k] + step_size * d[k]
        rs[k] = r[k] - step_size * a[k]
        ds[k] = g[k] - step_size * w[k] + ratio * d[k]
        for i, (src, dst) in enumerate(((xs, x_out), (rs, r_out), (ds, d_out))):
            write = pltpu.make_async_copy(src.at[k], dst.at[k], sem.at[i, k])
            write.start()
            writes.append(write)
    for write in writes:
        write.wait()


def local(T, S, solution, residual, direction, capacity):
    L, X, Y = capacity.shape
    field = jax.ShapeDtypeStruct((L, X, Y), jnp.float32)
    whole = pltpu.VMEM((L, X, Y), jnp.float32)
    halo = pltpu.VMEM((2, X, Y), jnp.float32)
    near, far = pl.BlockSpec(memory_space=pltpu.VMEM), pl.BlockSpec(memory_space=pltpu.HBM)
    kept = pl.pallas_call(
        functools.partial(exchange, T, S),
        out_shape=(field,) * 6 + (jax.ShapeDtypeStruct((8, Y), jnp.float32),),
        in_specs=[far] * 4,
        out_specs=(near,) * 7,
        scratch_shapes=[whole] * 5 + [halo] * 5 + [
            pltpu.VMEM((T * S, 4, Y), jnp.float32),
            pltpu.SemaphoreType.DMA((4,)),
            pltpu.SemaphoreType.DMA((4, L)),
            pltpu.SemaphoreType.DMA((4, L)),
            pltpu.SemaphoreType.DMA((3, 2)),
            pltpu.SemaphoreType.DMA((3, 2)),
            pltpu.SemaphoreType.DMA((T * S,)),
            pltpu.SemaphoreType.DMA((T * S,)),
            pltpu.SemaphoreType.REGULAR((T + S - 3,)),
        ],
        compiler_params=pltpu.CompilerParams(
            collective_id=0, has_side_effects=True, vmem_limit_bytes=53568 * 1024),
    )(solution[0], residual[0], direction[0], capacity)
    outs = pl.pallas_call(
        finish,
        out_shape=(field,) * 3,
        in_specs=[near] * 7,
        out_specs=(far,) * 3,
        scratch_shapes=[whole] * 3 + [pltpu.SemaphoreType.DMA((3, L))],
        compiler_params=pltpu.CompilerParams(vmem_limit_bytes=16 * 1024 * 1024),
    )(*kept)
    return tuple(out[None] for out in outs)


def solution(mesh):
    field = P(("groups", "tm"), "space", None, None)
    return jax.shard_map(
        functools.partial(local, mesh.shape["tm"], mesh.shape["space"]),
        mesh=mesh,
        in_specs=(field, field, field, P(("groups", "space"), None, None)),
        out_specs=(field, field, field),
        check_vma=False,
    )
```
